32 devices in a mesh: row: 4 (over y, core), col: 8 (over z, x).
Axes of the slice: x: 2, y: 2, z: 4, core: 2. Of those that a mesh axis runs over, the one named last changes fastest.
Arguments:
- tokens: bfloat16 [128, 8192], P('col', 'row'), may hold values from -120 to 120
- source: int32 [128], replicated, may hold values from 0 to 127, each once
- gain: float32 [8192], P('row'), may hold values from 0.5 to 1.5
- gate_weight: bfloat16 [8192, 29568], P('row', 'col'), may hold values from -0.0625 to 0.0625
- up_weight: bfloat16 [8192, 29568], P('row', 'col'), may hold values from -0.0625 to 0.0625
- down_weight: bfloat16 [29568, 8192], P('col', 'row'), may hold values from -0.03125 to 0.03125
Outputs:
- mixed: bfloat16 [128, 8192], P('col', 'row')
The draws below stay inside these ranges and needn't reach their ends.
All inputs are finite; a program needn't handle non-finite values.
Results may differ from the reference program's by a relative error of at most 0.0064.
Values may be sent and summed in bfloat16 or wider, within the bound.
A program may use at most 128 MiB of HBM per device.

```python
import jax
import jax.numpy as jnp
from jax import lax

D = 8192
FF = 29568
TOKENS = 128


def draw_tokens(key, part):
    first, second = jax.random.split(key, 2)
    position = jnp.arange(D, dtype=jnp.float32) / D
    column_scale = 10.0 ** position
    row_scale = 10.0 ** jax.random.uniform(first, (TOKENS, 1), dtype=jnp.float32)
    values = jnp.clip(jax.random.normal(second, (TOKENS, D), dtype=jnp.float32), -4.0, 4.0)
    return (0.3 * values * column_scale * row_scale).astype(jnp.bfloat16)


def shard_levels(own_key, extent, pieces, low, largest):
    def one(dim, blocks):
        draws = jax.random.uniform(jax.random.fold_in(jax.random.fold_in(own_key, 6), dim), (blocks,), jnp.float32, low / len(pieces), largest / len(pieces))
        return jnp.repeat(jnp.exp(draws), extent[dim] // blocks).reshape((-1,) + (1,) * (len(extent) - dim - 1))

    loudness = one(*pieces[0])
    for cut in pieces[1:]:
        loudness = loudness * one(*cut)
    return loudness


def scatter_about(stream_key, extent, scale, limit, pieces=(), kind=jnp.bfloat16):
    factor_of = shard_levels(stream_key, extent, pieces, -0.22, 0.18) if pieces else 1.0
    result = jax.random.normal(stream_key, extent, jnp.float32) * scale * factor_of
    return jnp.minimum(jnp.maximum(result, -limit), limit).astype(kind)


def setup_inputs(seed: int = 0) -> dict:
    keys = jax.random.split(jax.random.key(seed), 7)
    tokens = draw_tokens(jax.random.fold_in(keys[6], 71), 0)
    source = jax.random.permutation(keys[1], TOKENS).astype(jnp.int32)
    gain = jnp.clip(0.5 + 1.0 * jax.random.uniform(keys[2], (D,), jnp.float32) ** shard_levels(keys[2], (D,), ((0, 4),), -0.2, 0.2), 0.5, 1.5)
    gate_weight = scatter_about(keys[3], (D, FF), D ** -0.5, 0.0625, ((0, 4), (1, 8)))
    up_weight = scatter_about(keys[4], (D, FF), D ** -0.5, 0.0625, ((0, 4), (1, 8)))
    down_weight = scatter_about(keys[5], (FF, D), FF ** -0.5, 0.03125, ((0, 8), (1, 4)))
    return {"tokens": tokens, "source": source, "gain": gain, "gate_weight": gate_weight, "up_weight": up_weight, "down_weight": down_weight}


def reference(tokens, source, gain, gate_weight, up_weight, down_weight):
    merged = jnp.take(tokens, source, axis=0)
    wide = merged.astype(jnp.float32)
    squares = lax.optimization_barrier(jnp.sum(wide * wide, axis=1, keepdims=True))
    scale = lax.rsqrt(squares / D + 1e-06)
    weighted = (wide * gain).astype(jnp.bfloat16)
    gate = scale * jnp.dot(weighted, gate_weight, preferred_element_type=jnp.float32)
    up = scale * jnp.dot(weighted, up_weight, preferred_element_type=jnp.float32)
    hidden = (jax.nn.silu(gate) * up).astype(jnp.bfloat16)
    return jnp.dot(hidden, down_weight, preferred_element_type=jnp.float32).astype(jnp.bfloat16)
```

```python
import functools

import jax
import jax.numpy as jnp
from jax import lax
from jax.experimental import pallas as pl
from jax.experimental.pallas import tpu as pltpu
from jax.sharding import PartitionSpec as P

F32 = jnp.float32
BF16 = jnp.bfloat16
TILE = 256
CHUNK = 512
PIECES = 4


def chunks_of(width):
    count = max(1, -(-(width - TILE) // CHUNK))
    starts = [i * CHUNK for i in range(count)]
    ends = starts[1:] + [width]
    return [(a, b - a) for a, b in zip(starts, ends)]


def lanes(width):
    return -(-width // 128) * 128


def kernel(R, C, chunks, tok_ref, src_ref, gain_ref, wg_hbm, wu_hbm, wd_hbm, out_ref,
           wg, wu, wd, G, wt, sq_out, sq_in, part, sendA, recvA, own, sendB, recvB, H,
           acc, sendX, recvX, sendZ, recvZ,
           wg_sem, wu_sem, wd_sem, agz_s, agz_r, agx_s, agx_r, sq_s, sq_r,
           a_s, a_r, b_s, b_r, hy_s, hy_r, hs_s, hs_r, x_s, x_r, z_s, z_r):
    Y, Z = R // 2, C // 2
    T = wt.shape[0]
    Dl = wt.shape[1]
    S = T // R
    Tc = T // C
    n = len(chunks)
    r = lax.axis_index("row")
    c = lax.axis_index("col")
    y, k = r // 2, lax.rem(r, 2)
    z, x = c // 2, lax.rem(c, 2)
    sib = {"row": y * 2 + (1 - k)}
    mate = {"col": z * 2 + (1 - x)}

    def ynext(d):
        return lax.rem(y + d, Y)

    def znext(d):
        return lax.rem(z + d, Z)

    def remote(src, dst, s, rv, dev):
        return pltpu.make_async_remote_copy(
            src_ref=src, dst_ref=dst, send_sem=s, recv_sem=rv, device_id=dev,
            device_id_type=pl.DeviceIdType.MESH)

    loads = {"g": [], "u": [], "d": []}
    parts = wg_sem.shape[0]
    step = Dl // parts
    for name, hbm, vm, sem in (("g", wg_hbm, wg, wg_sem), ("u", wu_hbm, wu, wu_sem)):
        for i in range(parts):
            cp = pltpu.make_async_copy(hbm.at[pl.ds(i * step, step)], vm.at[pl.ds(i * step, step)], sem.at[i])
            cp.start()
            loads[name].append(cp)
    for i, (c0, w) in enumerate(chunks):
        cp = pltpu.make_async_copy(wd_hbm.at[pl.ds(c0, w)], wd.at[pl.ds(c0, w)], wd_sem.at[i])
        cp.start()
        loads["d"].append(cp)

    barrier = pltpu.get_barrier_semaphore()
    for d in range(1, R):
        pl.semaphore_signal(barrier, inc=1, device_id={"row": lax.rem(r + d, R)},
                            device_id_type=pl.DeviceIdType.MESH)
    for d in range(1, Z):
        pl.semaphore_signal(barrier, inc=1, device_id={"col": znext(d) * 2 + x},
                            device_id_type=pl.DeviceIdType.MESH)
    pl.semaphore_signal(barrier, inc=1, device_id=mate, device_id_type=pl.DeviceIdType.MESH)
    G[c] = tok_ref[...]
    pl.semaphore_wait(barrier, R - 1 + Z - 1 + 1)

    sent = []

    def ag_forward(d):
        block = lax.rem(z + Z - d, Z) * 2 + x
        cp = remote(G.at[block], G.at[block], agx_s.at[d], agx_r.at[d], mate)
        cp.start()
        sent.append(cp)
        return cp

    along = []
    for d in range(1, Z):
        cp = remote(G.at[c], G.at[c], agz_s.at[d - 1], agz_r.at[d - 1], {"col": znext(d) * 2 + x})
        cp.start()
        along.append(cp)
        sent.append(cp)
    across = [ag_forward(0)]
    order = sorted(range(1, Z), key=lambda d: min(d, Z - d))
    for d in order:
        along[d - 1].wait_recv()
        across.append(ag_forward(d))
    for cp in across:
        cp.wait_recv()

    pick = (src_ref[...] == lax.broadcasted_iota(jnp.int32, (T, T), 1)).astype(BF16)
    fw = min(512, Dl)
    total = jnp.zeros((T, 1), F32)
    for f in range(Dl // fw):
        cols = slice(f * fw, (f + 1) * fw)
        m = jnp.dot(pick, G[:, :, cols].reshape(T, fw), preferred_element_type=F32)
        total = total + jnp.sum(m * m, axis=1, keepdims=True)
        wt[:, cols] = (m * gain_ref[:, cols]).astype(BF16)
    sq_out[...] = jnp.broadcast_to(total, (T, 128)).reshape(R, S, 128)
    squares = []
    for d in range(1, R):
        to = lax.rem(r + d, R)
        cp = remote(sq_out.at[to], sq_in.at[d - 1], sq_s.at[d - 1], sq_r.at[d - 1], {"row": to})
        cp.start()
        squares.append(cp)
        sent.append(cp)

    copies = {}

    def product(u):
        j, s = u // 2, u % 2
        c0, w = chunks[j]
        W = wu if s else wg
        if u < 2:
            for cp in loads["u" if s else "g"]:
                cp.wait()
        full = w // TILE

        def body(t, _):
            off = pl.multiple_of(t * TILE, TILE)
            v = jnp.dot(wt[...], W[:, pl.ds(pl.multiple_of(c0 + off, TILE), TILE)], preferred_element_type=F32)
            part[s, :, :, pl.ds(off, TILE)] = v.reshape(R, S, TILE)
            return 0

        lax.fori_loop(0, full, body, 0)
        rest = w - full * TILE
        if rest:
            v = jnp.dot(wt[...], W[:, c0 + full * TILE:c0 + w], preferred_element_type=F32)
            part[s, :, :, full * TILE:w] = v.reshape(R, S, rest)
        wp = lanes(w)
        for yy in range(Y):
            sendA[j, s, yy, :, :w] = part[s, yy * 2 + (1 - k), :, :w].astype(BF16)
        cp = remote(sendA.at[j, s, :, :, pl.ds(0, wp)], recvA.at[j, s, :, :, pl.ds(0, wp)],
                    a_s.at[j, s], a_r.at[j, s], sib)
        cp.start()
        copies["a", u] = cp
        sent.append(cp)

    def pair_sum(u):
        j, s = u // 2, u % 2
        w = chunks[j][1]
        wp = lanes(w)
        copies["a", u].wait_recv()
        for d in range(1, Y):
            to = ynext(d)
            sendB[j, s, d - 1, :, :w] = (
                part[s, to * 2 + k, :, :w] + recvA[j, s, to, :, :w].astype(F32)).astype(BF16)
            cp = remote(sendB.at[j, s, d - 1, :, pl.ds(0, wp)], recvB.at[j, s, d - 1, :, pl.ds(0, wp)],
                        b_s.at[j, s, d - 1], b_r.at[j, s, d - 1], {"row": to * 2 + k})
            cp.start()
            copies["b", u, d] = cp
            sent.append(cp)
        own[j, s, :, :w] = part[s, r, :, :w] + recvA[j, s, y, :, :w].astype(F32)

    def hidden(j):
        w = chunks[j][1]
        wp = lanes(w)
        if j == 0:
            for cp in squares:
                cp.wait_recv()
        sq = sq_out[r]
        for d in range(1, R):
            sq = sq + sq_in[d - 1]
        scale = lax.rsqrt(sq[:, :1] / (Dl * R) + 1e-6)
        sums = []
        for s in range(2):
            v = own[j, s, :, :w]
            for d in range(1, Y):
                copies["b", 2 * j + s, d].wait_recv()
                v = v + recvB[j, s, d - 1, :, :w].astype(F32)
            sums.append(scale * v)
        gate, up = sums
        H[j, r, :, :w] = (gate / (1.0 + jnp.exp(-gate)) * up).astype(BF16)
        for d in range(1, Y):
            view = H.at[j, r, :, pl.ds(0, wp)]
            cp = remote(view, view, hy_s.at[j, d - 1], hy_r.at[j, d - 1], {"row": ynext(d) * 2 + k})
            cp.start()
            copies["hy", j, d] = cp
            sent.append(cp)
        to_sibling(j, 0)

    def to_sibling(j, d):
        wp = lanes(chunks[j][1])
        view = H.at[j, lax.rem(y + Y - d, Y) * 2 + k, :, pl.ds(0, wp)]
        cp = remote(view, view, hs_s.at[j, d], hs_r.at[j, d], sib)
        cp.start()
        copies["hs", j, d] = cp
        sent.append(cp)

    def forward(j):
        for d in range(1, Y):
            copies["hy", j, d].wait_recv()
            to_sibling(j, d)

    def down_cols(j, first, count):
        c0, w = chunks[j]
        tile = min(TILE, Dl // PIECES)

        def body(t, _):
            cols = pl.ds(pl.multiple_of(first + t * tile, 128), tile)
            v = jnp.dot(H[j, :, :, :w].reshape(T, w), wd[c0:c0 + w, cols], preferred_element_type=F32)
            v = v.reshape(C, Tc, tile)
            acc[:, :, cols] = v if j == 0 else acc[:, :, cols] + v
            return 0

        lax.fori_loop(0, count // tile, body, 0)

    def down_ready(j):
        for d in range(Y):
            copies["hs", j, d].wait_recv()
        loads["d"][j].wait()

    width = Dl // PIECES

    def send_across(p):
        cols = slice(p * width, (p + 1) * width)
        for zz in range(Z):
            sendX[p, zz] = acc[zz * 2 + (1 - x), :, cols].astype(BF16)
        cp = remote(sendX.at[p], recvX.at[p], x_s.at[p], x_r.at[p], mate)
        cp.start()
        copies["x", p] = cp
        sent.append(cp)

    def send_along(p):
        cols = slice(p * width, (p + 1) * width)
        copies["x", p].wait_recv()
        for d in sorted(range(1, Z), key=lambda d: -min(d, Z - d)):
            to = znext(d)
            sendZ[p, d - 1] = (acc[to * 2 + x, :, cols] + recvX[p, to].astype(F32)).astype(BF16)
            cp = remote(sendZ.at[p, d - 1], recvZ.at[p, d - 1], z_s.at[p, d - 1], z_r.at[p, d - 1],
                        {"col": to * 2 + x})
            cp.start()
            copies["z", p, d] = cp
            sent.append(cp)

    def finish(p):
        cols = slice(p * width, (p + 1) * width)
        v = acc[c, :, cols] + recvX[p, z].astype(F32)
        for d in range(1, Z):
            copies["z", p, d].wait_recv()
            v = v + recvZ[p, d - 1].astype(F32)
        out_ref[:, cols] = v.astype(BF16)

    for i in range(n + 4):
        for s in range(2):
            u = 2 * i + s
            if u < 2 * n:
                product(u)
            if 0 <= u - 1 < 2 * n:
                pair_sum(u - 1)
        if 0 <= i - 2 < n:
            hidden(i - 2)
        if 0 <= i - 3 < n:
            forward(i - 3)
        if 0 <= i - 4 < n - 1:
            down_ready(i - 4)
            down_cols(i - 4, 0, Dl)
    down_ready(n - 1)
    for p in range(PIECES):
        down_cols(n - 1, p * width, width)
        send_across(p)
        if p:
            send_along(p - 1)
    send_along(PIECES - 1)
    for p in range(PIECES):
        finish(p)
    for cp in sent:
        cp.wait_send()


def on_device(R, C, tokens, source, gain, gate_weight, up_weight, down_weight):
    Tc, Dl = tokens.shape
    T = Tc * C
    S = T // R
    Y, Z = R // 2, C // 2
    FL = gate_weight.shape[1]
    chunks = chunks_of(FL)
    n = len(chunks)
    wmax = max(lanes(w) for _, w in chunks)
    width = Dl // PIECES
    dma = pltpu.SemaphoreType.DMA
    vm = pltpu.VMEM
    loads = 4
    scratch = [
        vm((Dl, FL), BF16), vm((Dl, FL), BF16), vm((FL, Dl), BF16),
        vm((C, Tc, Dl), BF16), vm((T, Dl), BF16),
        vm((R, S, 128), F32), vm((R - 1, S, 128), F32),
        vm((2, R, S, wmax), F32),
        vm((n, 2, Y, S, wmax), BF16), vm((n, 2, Y, S, wmax), BF16),
        vm((n, 2, S, wmax), F32),
        vm((n, 2, Y - 1, S, wmax), BF16), vm((n, 2, Y - 1, S, wmax), BF16),
        vm((n, R, S, wmax), BF16),
        vm((C, Tc, Dl), F32),
        vm((PIECES, Z, Tc, width), BF16), vm((PIECES, Z, Tc, width), BF16),
        vm((PIECES, Z - 1, Tc, width), BF16), vm((PIECES, Z - 1, Tc, width), BF16),
        dma((loads,)), dma((loads,)), dma((n,)),
        dma((Z - 1,)), dma((Z - 1,)), dma((Z,)), dma((Z,)), dma((R - 1,)), dma((R - 1,)),
        dma((n, 2)), dma((n, 2)), dma((n, 2, Y - 1)), dma((n, 2, Y - 1)),
        dma((n, Y - 1)), dma((n, Y - 1)), dma((n, Y)), dma((n, Y)),
        dma((PIECES,)), dma((PIECES,)), dma((PIECES, Z - 1)), dma((PIECES, Z - 1)),
    ]
    vspec = pl.BlockSpec(memory_space=pltpu.VMEM)
    hspec = pl.BlockSpec(memory_space=pl.ANY)
    return pl.pallas_call(
        functools.partial(kernel, R, C, chunks),
        out_shape=jax.ShapeDtypeStruct((Tc, Dl), BF16),
        in_specs=[vspec, vspec, vspec, hspec, hspec, hspec],
        out_specs=vspec,
        scratch_shapes=scratch,
        compiler_params=pltpu.CompilerParams(
            collective_id=0, has_side_effects=True, vmem_limit_bytes=62 * 1024 * 1024),
        cost_estimate=pl.CostEstimate(
            flops=6 * T * Dl * FL, bytes_accessed=6 * Dl * FL, transcendentals=S * FL),
        name="feed_forward",
    )(tokens, source.reshape(T, 1), gain.reshape(1, Dl), gate_weight, up_weight, down_weight)


def solution(mesh):
    return jax.shard_map(
        functools.partial(on_device, mesh.shape["row"], mesh.shape["col"]),
        mesh=mesh,
        in_specs=(
            P("col", "row"),
            P(),
            P("row"),
            P("row", "col"),
            P("row", "col"),
            P("col", "row"),
        ),
        out_specs=P("col", "row"),
        check_vma=False,
    )
```
